256 devices in a mesh: gx: 16 (over y_lo, x, core), gy: 16 (over y_hi, z).
Axes of the slice: x: 4, y: 4 (y_hi: 2, y_lo: 2; y = y_hi * 2 + y_lo), z: 8, core: 2. Of those that a mesh axis runs over, the one named last changes fastest.
Arguments:
- labels: int32 [64, 256, 256], P('gx', 'gy'), may hold values from 0 to 7
- speed: float32 [8], replicated, may hold values from 0.9 to 2
- absorption: float32 [8], replicated, may hold values from 0.01 to 0.15
- amplitude: float32 [2, 16, 2], replicated, may hold values from -6 to 6
- source_x: int32 [2, 16], replicated, may hold values from 0 to 60
- source_y: int32 [2, 16], replicated, may hold values from 0 to 252
- source_z: int32 [2, 16], replicated, may hold values from 0 to 252
Outputs:
- field: float32 [2, 2, 64, 256, 256], P(None, None, 'gx', 'gy')
The draws below stay inside these ranges and needn't reach their ends.
Inputs may be any that keep to these rules, and one draw needn't show every extreme that they name: `labels`: indexes speed and absorption. `source_x`: each source block of 4 cells lies inside the grid. `source_y`: each source block of 4 cells lies inside the grid. `source_z`: each source block of 4 cells lies inside the grid.
All inputs are finite; a program needn't handle non-finite values.
Results may differ from the reference program's by a relative error of at most 0.00013.
Values sent between devices are 32-bit elements; how exact they have to be, the bound alone decides.
A program may use at most 64 MiB of HBM per device.

```python
import math
import jax
import jax.numpy as jnp
from jax import lax

NZ = 256
FIELDS = 2
NSRC = 16
SBLK = 4
LABELS = 8
ITERS = 4
NX = 64
NY = 256


def set_ends(values, rng, smallest, top_value):
    place = [jax.random.randint(jax.random.fold_in(rng, axis), (), 0, length) for axis, length in enumerate(values.shape)]
    longest = values.shape.index(max(values.shape))
    beside = place[:longest] + [(place[longest] + 1) % values.shape[longest]] + place[longest + 1:]
    return values.at[tuple(place)].set(smallest).at[tuple(beside)].set(top_value)


def normal_values(rng, extent, scale, bound, held_as=jnp.bfloat16):
    array = scale * jax.random.normal(rng, extent, jnp.float32)
    return jnp.clip(array, min=-bound, max=bound).astype(held_as)


def setup_inputs(seed: int = 0) -> dict:
    splits = jax.random.split(jax.random.key(seed), 8)
    return {
        "labels": set_ends(jax.random.randint(splits[0], (NX, NY, NZ), 0, LABELS), jax.random.fold_in(splits[0], 1), 0, LABELS - 1).astype(jnp.int32),
        "speed": jnp.clip(jnp.exp(jax.random.uniform(splits[1], (LABELS,), jnp.float32, math.log(0.9), math.log(2.0))), 0.9, 2.0),
        "absorption": jnp.clip(jax.random.uniform(splits[2], (LABELS,), jnp.float32, 0.01, 0.15), 0.01, 0.15),
        "amplitude": normal_values(splits[3], (FIELDS, NSRC, 2), 1.0, 6.0, jnp.float32),
        "source_x": set_ends(jax.random.randint(splits[4], (FIELDS, NSRC), 0, NX - SBLK + 1), jax.random.fold_in(splits[4], 1), 0, NX - SBLK).astype(jnp.int32),
        "source_y": set_ends(jax.random.randint(splits[5], (FIELDS, NSRC), 0, NY - SBLK + 1), jax.random.fold_in(splits[5], 1), 0, NY - SBLK).astype(jnp.int32),
        "source_z": set_ends(jax.random.randint(splits[6], (FIELDS, NSRC), 0, NZ - SBLK + 1), jax.random.fold_in(splits[6], 1), 0, NZ - SBLK).astype(jnp.int32),
    }


wave_number = 2.0 * math.pi / 6.0
highest = lax.Precision.HIGHEST

def medium_table(speed, absorption):
    real_k = wave_number / speed
    table_real = real_k * real_k - absorption * absorption
    table_imag = 2.0 * real_k * absorption
    centre = 0.5 * (jnp.min(table_real) + jnp.max(table_real))
    spread = 1.05 * jnp.max(jnp.sqrt((table_real - centre) ** 2 + table_imag ** 2))
    return (table_real, table_imag, centre, spread)

def smoothed(values):
    beside_all = jnp.zeros_like(values)
    for axis in range(3):
        beside_all = beside_all + jnp.roll(values, 1, axis) + jnp.roll(values, -1, axis)
    return 0.5 * values + beside_all / 12.0

def block_mask(corner, length):
    cells = jnp.arange(length, dtype=jnp.int32)
    inside = (cells[None, None, :] >= corner[:, :, None]) & (cells[None, None, :] < corner[:, :, None] + SBLK)
    return inside.astype(jnp.float32)

def squared_wave(length):
    index = jnp.arange(length, dtype=jnp.int32)
    folded = jnp.where(index < length // 2, index, index - length).astype(jnp.float32)
    wave = 2.0 * math.pi * folded / length
    return wave * wave

def reference(labels, speed, absorption, amplitude, source_x, source_y, source_z):
    table_real, table_imag, centre, spread = medium_table(speed, absorption)
    ksq_real = jnp.zeros(labels.shape, jnp.float32)
    ksq_imag = jnp.zeros(labels.shape, jnp.float32)
    for label in range(LABELS):
        hit = labels == label
        ksq_real = jnp.where(hit, table_real[label], ksq_real)
        ksq_imag = jnp.where(hit, table_imag[label], ksq_imag)
    pot_real = smoothed(ksq_real) - centre
    pot_imag = smoothed(ksq_imag) - spread
    potential = pot_real + 1j * pot_imag
    gain = 1j * potential / spread
    mask_x = block_mask(source_x, NX)
    mask_y = block_mask(source_y, NY)
    mask_z = block_mask(source_z, NZ)
    first = jnp.einsum('fsc,fsx->fcsx', amplitude, mask_x, precision=highest)
    second = jnp.einsum('fcsx,fsy->fcsxy', first, mask_y, precision=highest)
    source = jnp.einsum('fcsxy,fsz->fcxyz', second, mask_z, precision=highest)
    source_c = source[:, 0] + 1j * source[:, 1]
    wave_sq = squared_wave(NX)[:, None, None] + squared_wave(NY)[None, :, None] + squared_wave(NZ)[None, None, :]
    green = 1.0 / (wave_sq - centre - 1j * spread)
    field = 0.0 * source_c
    for iteration in range(ITERS):
        rhs = potential * field + source_c
        scattered = jnp.fft.ifftn(jnp.fft.fftn(rhs, axes=(1, 2, 3)) * green, axes=(1, 2, 3))
        field = field + gain * (scattered - field)
    return jnp.stack([jnp.real(field), jnp.imag(field)], axis=1).astype(jnp.float32)
```

```python
import functools
import math

import jax
import jax.numpy as jnp
import numpy as np
from jax import lax
from jax.experimental import pallas as pl
from jax.experimental.pallas import tpu as pltpu
from jax.sharding import PartitionSpec as P

ITERS = 4
GROUP = 16
MESH = pl.DeviceIdType.MESH
F32 = jnp.float32
BF16 = jnp.bfloat16
WAVE = 2.0 * math.pi / 6.0
GX_OUT, GY_OUT, GY_BACK, GX_BACK = range(4)


def transform_matrices():
    n = np.arange(128)
    phase = 2.0 * np.pi * (np.outer(n, n) % 128) / 128
    c, s = np.cos(phase), np.sin(phase)
    z_out = np.block([[c, s], [-s, c]])
    z_back = np.block([[c, -s], [s, c]])
    order = (np.arange(2)[None, :, None] * 128 + np.arange(16)[:, None, None] * 8 + np.arange(8)).reshape(-1)
    z_out = z_out[order]
    z_back = z_back[:, order]
    p, a, b = n >> 6, (n >> 4) & 3, n & 15
    phase = 2.0 * np.pi * ((4 * np.outer(a, a) + np.outer(b, b)) % 16) / 16
    same = p[:, None] == p[None, :]
    c, s = np.cos(phase) * same, np.sin(phase) * same
    xy_out = np.block([[c, -s], [s, c]])
    xy_back = np.block([[c, s], [-s, c]])
    parts = []
    for matrix in (z_out, z_back, xy_out, xy_back):
        high = matrix.astype(BF16)
        parts.append(high)
        parts.append((matrix - high.astype(np.float64)).astype(BF16))
    return np.stack(parts)


def cos_turn(m):
    m = m & 255
    t = (64 - jnp.minimum(m, 256 - m)).astype(F32) * (2.0 * math.pi / 256)
    q = t * t
    poly = -1.0 / 39916800
    for term in (1.0 / 362880, -1.0 / 5040, 1.0 / 120, -1.0 / 6, 1.0):
        poly = poly * q + term
    return t * poly


def backward_turn(m):
    return cos_turn(m), -cos_turn(m - 64)


def cmul(a, b):
    return a[0] * b[0] - a[1] * b[1], a[0] * b[1] + a[1] * b[0]


def cmul_conj(a, b):
    return a[0] * b[0] + a[1] * b[1], a[1] * b[0] - a[0] * b[1]


def box_sum(m):
    w = backward_turn(m)
    square = backward_turn(2 * m)
    return cmul((1.0 + w[0], w[1]), (1.0 + square[0], square[1]))


def dft4(a, sign):
    (r0, i0), (r1, i1), (r2, i2), (r3, i3) = a
    sr, si, dr, di = r0 + r2, i0 + i2, r0 - r2, i0 - i2
    tr, ti, ur, ui = r1 + r3, i1 + i3, r1 - r3, i1 - i3
    minus, plus = (dr + ui, di - ur), (dr - ui, di + ur)
    if sign > 0:
        minus, plus = plus, minus
    return [(sr + tr, si + ti), minus, (sr - tr, si - ti), plus]


def turn16(a, m, sign):
    if m == 0:
        return a
    r, i = a
    if m == 4:
        return (i, -r) if sign < 0 else (-i, r)
    c, s = math.cos(2 * math.pi * m / 16), sign * math.sin(2 * math.pi * m / 16)
    if m == 2 or m == 6:
        return _rot((r - i) * math.sqrt(0.5), (r + i) * math.sqrt(0.5), c, s)
    return r * c - i * s, r * s + i * c


def _rot(minus, plus, c, s):
    if c > 0 and s > 0:
        return minus, plus
    if c > 0:
        return plus, -minus
    if s > 0:
        return -plus, minus
    return -minus, -plus


def dft16(x, sign):
    inner = [dft4([x[4 * n1 + n2] for n1 in range(4)], sign) for n2 in range(4)]
    out = [None] * 16
    for k1 in range(4):
        column = [turn16(inner[n2][k1], n2 * k1, sign) for n2 in range(4)]
        for k2, value in enumerate(dft4(column, sign)):
            out[k1 + 4 * k2] = value
    return out


def split(x):
    high = x.astype(BF16)
    return high, (x - high.astype(F32)).astype(BF16)


def matmul(a, b):
    dot = functools.partial(jnp.dot, preferred_element_type=F32)
    return dot(a[0], b[0]) + (dot(a[0], b[1]) + dot(a[1], b[0]))


def lane_parts(lane):
    return lane >> 6, (lane >> 4) & 3, lane & 15


def swap_halves(t, sign):
    return pltpu.roll(t, 64, 1) + sign * t


def folded_square(index, length):
    wave = 2.0 * math.pi * jnp.where(index < length // 2, index, index - length).astype(F32) / length
    return wave * wave


def medium(speed, absorption):
    k = WAVE / speed
    real = k * k - absorption * absorption
    imag = 2.0 * k * absorption
    centre = 0.5 * (jnp.min(real, axis=1, keepdims=True) + jnp.max(real, axis=1, keepdims=True))
    size = jnp.sqrt((real - centre) ** 2 + imag * imag)
    return real, imag, centre, 1.05 * jnp.max(size, axis=1, keepdims=True)


def look_up(labels, table):
    out = jnp.broadcast_to(table[:, 0:1], labels.shape)
    for l in range(1, table.shape[1]):
        out = jnp.where(labels == l, table[:, l : l + 1], out)
    return out


def column(row):
    n = row.shape[1]
    eye = lax.broadcasted_iota(jnp.int32, (n, n), 0) == lax.broadcasted_iota(jnp.int32, (n, n), 1)
    spread_out = jnp.where(eye, jnp.broadcast_to(row.astype(F32), (n, n)), 0.0)
    return jnp.sum(spread_out, axis=1, keepdims=True)


def to_lanes(a):
    return jnp.concatenate([a[:, :128], a[:, 128:]], axis=0).T


def from_lanes(a):
    a = a.T
    return jnp.concatenate([a[:64], a[64:]], axis=1)


def smoothed(own, x_low, x_high, y_low, y_high):
    row = lax.broadcasted_iota(jnp.int32, own.shape, 0) & 15

    def per_x(edge):
        return jnp.concatenate([jnp.broadcast_to(edge[x : x + 1], (16, 256)) for x in range(4)], axis=0)

    total = jnp.concatenate([x_low, own[:48]], axis=0) + jnp.concatenate([own[16:], x_high], axis=0)
    total = total + jnp.where(row == 0, per_x(y_low), pltpu.roll(own, 1, 0))
    total = total + jnp.where(row == 15, per_x(y_high), pltpu.roll(own, 63, 0))
    total = total + pltpu.roll(own, 1, 1) + pltpu.roll(own, 255, 1)
    return 0.5 * own + total * (1.0 / 12.0)


def source_spectrum(amplitude, sx, sy, sz, gx, gy):
    lane = lax.broadcasted_iota(jnp.int32, (16, 128), 1)
    parity, x2, y2 = lane_parts(lane)
    row_phase = sy * (lane >> 3) + sz * (16 * gx + 2 * (lane & 7))
    pr, pi = backward_turn(row_phase)
    qr, qi = cmul(backward_turn(4 * sx * (gy + 16 * x2) + 16 * sy * y2 + sz * parity), amplitude)
    left = jnp.concatenate([pr, pi], axis=0)
    right = jnp.concatenate(
        [jnp.concatenate([qr, qi], axis=1), jnp.concatenate([-qi, qr], axis=1)], axis=0
    )
    return lax.dot_general(
        left.T, right, (((1,), (0,)), ((), ())), precision=lax.Precision.HIGHEST, preferred_element_type=F32
    )


def kernel(
    labels, speed, absorption, amplitude, source_x, source_y, source_z, matrix_hbm, out,
    matrix, send, recv, field, first, potential, turns, wturn, green, edge, near_x, near_y,
    matrix_sem, send_sem, recv_sem, edge_send, edge_recv,
):
    gx, gy = lax.axis_index("gx"), lax.axis_index("gy")

    load = pltpu.make_async_copy(matrix_hbm, matrix, matrix_sem)
    load.start()

    barrier = pltpu.get_barrier_semaphore()

    def greet(step, carry):
        pl.semaphore_signal(barrier, inc=1, device_id=(lax.rem(gx + step, GROUP), gy), device_id_type=MESH)
        pl.semaphore_signal(barrier, inc=1, device_id=(gx, lax.rem(gy + step, GROUP)), device_id_type=MESH)
        return carry

    lax.fori_loop(1, GROUP, greet, 0)

    def start(stage, f):
        along_x = stage in (GX_OUT, GX_BACK)
        me = gx if along_x else gy

        def one(step, carry):
            to = lax.rem(me + step, GROUP)
            pltpu.make_async_remote_copy(
                src_ref=send.at[stage, f, to],
                dst_ref=recv.at[stage, f, me],
                send_sem=send_sem.at[stage, f],
                recv_sem=recv_sem.at[stage, f],
                device_id=(to, gy) if along_x else (gx, to),
                device_id_type=MESH,
            ).start()
            return carry

        lax.fori_loop(1, GROUP, one, 0)
        recv[stage, f, me] = send[stage, f, me]

    def all_but_one(ref, stage, f, sem):
        part = ref.at[stage, f, pl.ds(0, GROUP - 1)]
        return pltpu.make_async_copy(part, part, sem.at[stage, f])

    def arrived(stage, f):
        all_but_one(recv, stage, f, recv_sem).wait()

    def sent(stage, f):
        all_but_one(send, stage, f, send_sem).wait()

    def blocks(stage, f):
        return [(recv[stage, f, g, 0:8], recv[stage, f, g, 8:16]) for g in range(GROUP)]

    def put(stage, f, values):
        for g, (real, imag) in enumerate(values):
            send[stage, f, g, 0:8] = real
            send[stage, f, g, 8:16] = imag

    def rows(values):
        return jnp.concatenate(
            [jnp.concatenate([v[0] for v in values], axis=0), jnp.concatenate([v[1] for v in values], axis=0)], axis=1
        )

    def unrows(values):
        return [(values[8 * g : 8 * g + 8, :128], values[8 * g : 8 * g + 8, 128:]) for g in range(GROUP)]

    def turn_row(g):
        return turns[0, g : g + 1], turns[1, g : g + 1]

    def y_back(f, spectrum):
        mixed = unrows(matmul(split(rows(spectrum)), (matrix[6], matrix[7])))
        put(GY_BACK, f, dft16([cmul_conj(v, turn_row(g)) for g, v in enumerate(mixed)], 1))
        start(GY_BACK, f)

    def y_both(f):
        values = dft16(blocks(GY_OUT, f), -1)
        values = [cmul(v, turn_row(g)) for g, v in enumerate(values)]
        mixed = unrows(matmul(split(rows(values)), (matrix[4], matrix[5])))
        y_back(f, [cmul(v, (green[0, g], green[1, g])) for g, v in enumerate(mixed)])

    def x_out(f):
        put(GY_OUT, f, dft16(blocks(GX_OUT, f), -1))
        start(GY_OUT, f)

    def x_back(f):
        put(GX_BACK, f, dft16(blocks(GY_BACK, f), 1))
        start(GX_BACK, f)

    lane = lax.broadcasted_iota(jnp.int32, (128, 128), 1)
    half = jnp.where(lane < 64, 1.0, -1.0).astype(F32)

    def z_out(f):
        v = cmul((potential[0], potential[1]), (field[f, 0], field[f, 1]))
        v = cmul((swap_halves(v[0], half), swap_halves(v[1], half)), (wturn[0], wturn[1]))
        values = matmul((matrix[0], matrix[1]), split(jnp.concatenate(v, axis=0)))
        send[GX_OUT, f] = values.reshape(GROUP, 16, 128)
        start(GX_OUT, f)

    def z_back(f):
        values = matmul((matrix[2], matrix[3]), split(recv[GX_BACK, f].reshape(256, 128)))
        v = cmul_conj((values[:128], values[128:]), (wturn[0], wturn[1]))
        return swap_halves(v[0], half), swap_halves(v[1], half)

    def change_of(c, inverse):
        w = cmul((potential[0], potential[1]), c)
        return -w[1] * inverse, w[0] * inverse

    table_real, table_imag, centre, spread = medium(speed[...], absorption[...])
    inverse = 1.0 / spread

    lane16 = lax.broadcasted_iota(jnp.int32, (16, 128), 1)
    row16 = lax.broadcasted_iota(jnp.int32, (16, 128), 0)
    _, x16, y16 = lane_parts(lane16)
    turns[0], turns[1] = backward_turn(y16 * row16 + 4 * x16 * gy)
    lane8 = lax.broadcasted_iota(jnp.int32, (8, 128), 1)
    row8 = lax.broadcasted_iota(jnp.int32, (8, 128), 0)
    parity, x2, y2 = lane_parts(lane8)
    kx = gy + 16 * x2
    kz = 2 * (8 * gx + row8) + parity
    ky = row16 + 16 * y16
    beside = folded_square(kx, 64) + folded_square(kz, 256)
    wave_y = folded_square(ky, 256)
    box_xz = cmul(box_sum(4 * kx), box_sum(kz))
    box_y = box_sum(ky)
    scale = 1.0 / (64 * 256 * 256)
    weights = []
    for g in range(GROUP):
        shifted = (beside + wave_y[g : g + 1]) - centre
        share = scale / (shifted * shifted + spread * spread)
        value = (shifted * share, spread * share)
        green[0, g], green[1, g] = value
        weights.append(cmul(cmul(value, (box_y[0][g : g + 1], box_y[1][g : g + 1])), box_xz))
    load.wait()

    for x in range(4):
        edge[x : x + 1] = labels[x, 0:1]
        edge[4 + x : 5 + x] = labels[x, 15:16]

    spectra = []
    for f in range(2):
        amp = (amplitude[f, :, 0:1], amplitude[f, :, 1:2])
        corner = [column(s[f : f + 1]).astype(jnp.int32) for s in (source_x, source_y, source_z)]
        spectrum = unrows(source_spectrum(amp, *corner, gx, gy))
        spectra.append([cmul(v, w) for v, w in zip(spectrum, weights)])

    pl.semaphore_wait(barrier, 2 * (GROUP - 1))
    for f in range(2):
        y_back(f, spectra[f])

    up_x, down_x = lax.rem(gx + 1, GROUP), lax.rem(gx + GROUP - 1, GROUP)
    up_y, down_y = lax.rem(gy + 1, GROUP), lax.rem(gy + GROUP - 1, GROUP)
    edges = [
        pltpu.make_async_remote_copy(
            src_ref=source, dst_ref=target, send_sem=edge_send.at[k], recv_sem=edge_recv.at[k],
            device_id=device, device_id_type=MESH,
        )
        for k, (source, target, device) in enumerate(
            (
                (labels.at[3], near_x.at[0], (up_x, gy)),
                (labels.at[0], near_x.at[1], (down_x, gy)),
                (edge, near_y.at[0], (gx, up_y)),
                (edge, near_y.at[1], (gx, down_y)),
            )
        )
    ]
    for copy in edges:
        copy.start()

    z_low = lax.broadcasted_iota(jnp.int32, (128, 128), 0)
    wturn[0], wturn[1] = backward_turn(jnp.where(lane < 64, 0, z_low))
    for copy in edges:
        copy.wait()
    own = labels[...].reshape(64, 256)
    for part, (table, shift) in enumerate(((table_real, centre), (table_imag, spread))):
        values = [look_up(a, table) for a in (own, near_x[0], near_x[1], near_y[0, 4:8], near_y[1, 0:4])]
        potential[part] = to_lanes(smoothed(*values) - shift)

    for f in range(2):
        arrived(GY_BACK, f)
        x_back(f)
    for f in range(2):
        arrived(GX_BACK, f)
        v = z_back(f)
        first[f, 0], first[f, 1] = v
        field[f, 0], field[f, 1] = change_of(v, inverse)
        z_out(f)

    def iteration(step, carry):
        for f in range(2):
            arrived(GX_OUT, f)

            @pl.when(step > 0)
            def _():
                sent(GY_OUT, f)

            x_out(f)
        for f in range(2):
            arrived(GY_OUT, f)
            sent(GY_BACK, f)
            y_both(f)
        for f in range(2):
            arrived(GY_BACK, f)
            sent(GX_BACK, f)
            x_back(f)
        for f in range(2):
            arrived(GX_BACK, f)
            v = z_back(f)
            real, imag = field[f, 0], field[f, 1]
            move = change_of((v[0] + first[f, 0] - real, v[1] + first[f, 1] - imag), inverse)
            field[f, 0], field[f, 1] = real + move[0], imag + move[1]

            @pl.when(step < ITERS - 2)
            def _():
                sent(GX_OUT, f)
                z_out(f)

        return carry

    lax.fori_loop(0, ITERS - 1, iteration, 0)

    for f in range(2):
        for part in range(2):
            out[f, part] = from_lanes(field[f, part]).reshape(4, 16, 256)
    for stage in range(4):
        for f in range(2):
            sent(stage, f)


def per_device(labels, speed, absorption, amplitude, source_x, source_y, source_z):
    vmem = pl.BlockSpec(memory_space=pltpu.VMEM)
    return pl.pallas_call(
        kernel,
        out_shape=jax.ShapeDtypeStruct((2, 2, 4, 16, 256), F32),
        in_specs=[vmem] * 7 + [pl.BlockSpec(memory_space=pl.ANY)],
        out_specs=vmem,
        scratch_shapes=[
            pltpu.VMEM((8, 256, 256), BF16),
            pltpu.VMEM((4, 2, GROUP, 16, 128), F32),
            pltpu.VMEM((4, 2, GROUP, 16, 128), F32),
            pltpu.VMEM((2, 2, 128, 128), F32),
            pltpu.VMEM((2, 2, 128, 128), F32),
            pltpu.VMEM((2, 128, 128), F32),
            pltpu.VMEM((2, 16, 128), F32),
            pltpu.VMEM((2, 128, 128), F32),
            pltpu.VMEM((2, GROUP, 8, 128), F32),
            pltpu.VMEM((8, 256), jnp.int32),
            pltpu.VMEM((2, 16, 256), jnp.int32),
            pltpu.VMEM((2, 8, 256), jnp.int32),
            pltpu.SemaphoreType.DMA,
            pltpu.SemaphoreType.DMA((4, 2)),
            pltpu.SemaphoreType.DMA((4, 2)),
            pltpu.SemaphoreType.DMA((4,)),
            pltpu.SemaphoreType.DMA((4,)),
        ],
        compiler_params=pltpu.CompilerParams(
            collective_id=0, has_side_effects=True, vmem_limit_bytes=32 * 1024 * 1024
        ),
    )(
        labels,
        speed.reshape(1, 8),
        absorption.reshape(1, 8),
        amplitude,
        source_x,
        source_y,
        source_z,
        jnp.asarray(transform_matrices()),
    )


def solution(mesh):
    return jax.shard_map(
        per_device,
        mesh=mesh,
        in_specs=(P("gx", "gy", None), P(), P(), P(), P(), P(), P()),
        out_specs=P(None, None, "gx", "gy", None),
        check_vma=False,
    )
```

```python
import functools
import math

import jax
import jax.numpy as jnp
import numpy as np
from jax import lax
from jax.experimental import pallas as pl
from jax.experimental.pallas import tpu as pltpu
from jax.sharding import PartitionSpec as P

ITERS = 4
CHIPS = 128
MESH = pl.DeviceIdType.MESH
F32 = jnp.float32
BF16 = jnp.bfloat16
WAVE = 2.0 * math.pi / 6.0
OUT, BACK = range(2)


def transform_matrices():
    def both(phase):
        c, s = np.cos(2.0 * np.pi * phase), np.sin(2.0 * np.pi * phase)
        return np.block([[c, s], [-s, c]]), np.block([[c, -s], [s, c]])

    n = np.arange(128)
    pairs = (np.arange(2)[None, :] * 128 + n[:, None]).reshape(-1)
    z_out, z_back = both((np.outer(n, n) % 128) / 128)
    high, low = n >> 4, n & 15
    mixed = ((2 * np.outer(high, high) + np.outer(low, low)) % 16) / 16
    far_out, far_back = both(mixed)
    near_back, near_out = both(mixed)
    parts = []
    for matrix in (z_out[pairs], z_back[:, pairs], far_out[:, pairs], far_back[pairs], near_out, near_back):
        high = matrix.astype(BF16)
        parts.append(high)
        parts.append((matrix - high.astype(np.float64)).astype(BF16))
    return np.stack(parts)


def constant_tables():
    n = np.arange(128)
    row, lane = n[:, None], n[None, :]
    z_turn = np.exp(-2j * np.pi * row / 256) * np.ones((1, 128))
    xy_turn = np.exp(-2j * np.pi * ((row >> 4) * (lane >> 4) / 64 + (row & 15) * (lane & 15) / 256))
    kx, ky = (row >> 4) + 8 * (lane >> 4), (row & 15) + 16 * (lane & 15)
    box = sum(np.exp(-2j * np.pi * j * kx / 64) for j in range(4)) * sum(np.exp(-2j * np.pi * j * ky / 256) for j in range(4))
    wave = [
        (2.0 * np.pi * np.where(k < size // 2, k, k - size) / size).astype(np.float32) for k, size in ((kx, 64), (ky, 256))
    ]
    tables = [z_turn.real, z_turn.imag, xy_turn.real, xy_turn.imag, box.real, box.imag]
    return np.stack([t.astype(np.float32) for t in tables] + [wave[0] * wave[0] + wave[1] * wave[1]])


def cos_turn(m):
    m = m & 255
    t = (64 - jnp.minimum(m, 256 - m)).astype(F32) * (2.0 * math.pi / 256)
    q = t * t
    poly = -1.0 / 39916800
    for term in (1.0 / 362880, -1.0 / 5040, 1.0 / 120, -1.0 / 6, 1.0):
        poly = poly * q + term
    return t * poly


def backward_turn(m):
    return cos_turn(m), -cos_turn(m - 64)


def cmul(a, b):
    return a[0] * b[0] - a[1] * b[1], a[0] * b[1] + a[1] * b[0]


def cmul_conj(a, b):
    return a[0] * b[0] + a[1] * b[1], a[1] * b[0] - a[0] * b[1]


def box_sum(m):
    w = backward_turn(m)
    square = backward_turn(2 * m)
    return cmul((1.0 + w[0], w[1]), (1.0 + square[0], square[1]))


def split(x):
    high = x.astype(BF16)
    return high, (x - high.astype(F32)).astype(BF16)


def matmul(a, b):
    dot = functools.partial(jnp.dot, preferred_element_type=F32)
    return dot(a[0], b[0]) + (dot(a[0], b[1]) + dot(a[1], b[0]))


def medium(speed, absorption):
    k = WAVE / speed
    real = k * k - absorption * absorption
    imag = 2.0 * k * absorption
    centre = 0.5 * (jnp.min(real, axis=1, keepdims=True) + jnp.max(real, axis=1, keepdims=True))
    size = jnp.sqrt((real - centre) ** 2 + imag * imag)
    return real, imag, centre, 1.05 * jnp.max(size, axis=1, keepdims=True)


def look_up(labels, table):
    out = jnp.broadcast_to(table[:, 0:1], labels.shape)
    for l in range(1, table.shape[1]):
        out = jnp.where(labels == l, table[:, l : l + 1], out)
    return out


def column(row):
    n = row.shape[1]
    eye = lax.broadcasted_iota(jnp.int32, (n, n), 0) == lax.broadcasted_iota(jnp.int32, (n, n), 1)
    spread_out = jnp.where(eye, jnp.broadcast_to(row.astype(F32), (n, n)), 0.0)
    return jnp.sum(spread_out, axis=1, keepdims=True)


def smoothed(own, x_low, x_high, y_low, y_high):
    row = lax.broadcasted_iota(jnp.int32, own.shape, 0) & 15

    def per_x(edge):
        return jnp.concatenate([jnp.broadcast_to(edge[x : x + 1], (16, 256)) for x in range(8)], axis=0)

    total = jnp.concatenate([x_low, own[:112]], axis=0) + jnp.concatenate([own[16:], x_high], axis=0)
    total = total + jnp.where(row == 0, per_x(y_low), pltpu.roll(own, 1, 0))
    total = total + jnp.where(row == 15, per_x(y_high), pltpu.roll(own, 127, 0))
    total = total + pltpu.roll(own, 1, 1) + pltpu.roll(own, 255, 1)
    return 0.5 * own + total * (1.0 / 12.0)


def farthest_first():
    offsets = [(y, x, z) for y in range(4) for x in range(4) for z in range(8)][1:]
    return sorted(offsets, key=lambda o: -(min(o[0], 4 - o[0]) + min(o[1], 4 - o[1]) + min(o[2], 8 - o[2])))


def kernel(
    labels_hbm, speed_hbm, absorption_hbm, amplitude_hbm, sx_hbm, sy_hbm, sz_hbm, matrix_hbm, table_hbm, out,
    speed, absorption, amplitude, sx, sy, sz, matrix, table,
    labels, near_x, near_y, edge, potential, field, first, green, spectrum, result, send, recv,
    load_sem, send_sem, recv_sem, edge_send, edge_recv, half_send, half_recv,
):
    gx, gy = lax.axis_index("gx"), lax.axis_index("gy")
    core, chip_x = lax.rem(gx, 2), gx // 2
    me = chip_x * 16 + gy
    sibling = chip_x * 2 + 1 - core
    next_x, last_x = lax.rem(chip_x + 1, 8), lax.rem(chip_x + 7, 8)
    next_y, last_y = lax.rem(gy + 1, 16), lax.rem(gy + 15, 16)

    loads = [
        pltpu.make_async_copy(source, target, load_sem.at[k])
        for k, (source, target) in enumerate(
            (
                (labels_hbm, labels.at[pl.ds(4 * core, 4)]),
                (speed_hbm, speed),
                (absorption_hbm, absorption),
                (amplitude_hbm, amplitude),
                (sx_hbm, sx),
                (sy_hbm, sy),
                (sz_hbm, sz),
                (table_hbm, table),
                (matrix_hbm, matrix),
            )
        )
    ]
    for load in loads:
        load.start()

    place_y, place_x, place_z = 2 * (gy // 8) + gx // 8, lax.rem(chip_x, 4), lax.rem(gy, 8)
    ys = [lax.rem(place_y + d, 4) for d in range(4)]
    xs = [lax.rem(place_x + d, 4) for d in range(4)]
    zs = [lax.rem(place_z + d, 8) for d in range(8)]
    to_x = [[lax.rem(y, 2) * 4 + x for x in xs] for y in ys]
    to_y = [[(y // 2) * 8 + z for z in zs] for y in ys]
    order = farthest_first()

    barrier = pltpu.get_barrier_semaphore()

    def greet(device):
        pl.semaphore_signal(barrier, inc=1, device_id=device, device_id_type=MESH)

    for y, x, z in order:
        greet((2 * to_x[y][x] + core, to_y[y][z]))
    greet((sibling, gy))
    greet((2 * next_x + 1 - core, gy))
    greet((2 * last_x + 1 - core, gy))
    greet((sibling, next_y))
    greet((sibling, last_y))

    def start(stage, p):
        target = recv.at[stage, p, pl.ds(2 * me, 2)]
        for y, x, z in order:
            pltpu.make_async_remote_copy(
                src_ref=send.at[stage, p, pl.ds(2 * (to_x[y][x] * 16 + to_y[y][z]), 2)],
                dst_ref=target,
                send_sem=send_sem.at[stage, p],
                recv_sem=recv_sem.at[stage, p],
                device_id=(2 * to_x[y][x] + core, to_y[y][z]),
                device_id_type=MESH,
            ).start()
        pltpu.make_async_copy(send.at[stage, p, pl.ds(2 * me, 2)], target, recv_sem.at[stage, p]).start()

    def arrived(stage, p):
        whole = recv.at[stage, p]
        pltpu.make_async_copy(whole, whole, recv_sem.at[stage, p]).wait()

    def sent(stage, p):
        part = send.at[stage, p, pl.ds(0, 2 * CHIPS - 2)]
        pltpu.make_async_copy(part, part, send_sem.at[stage, p]).wait()

    def weights(k):
        return matrix[2 * k], matrix[2 * k + 1]

    def turns(k):
        return table[2 * k], table[2 * k + 1]

    def halves(a):
        return a[:128], a[128:]

    def sides(a):
        return a[:, :128], a[:, 128:]

    def beside(v):
        return jnp.concatenate(v, axis=1)

    def below(v):
        return jnp.concatenate(v, axis=0)

    for load in loads[1:8]:
        load.wait()
    table_real, table_imag, centre, spread = medium(speed[...], absorption[...])
    inverse = 1.0 / spread

    def pick(ref):
        return column(jnp.where(core == 0, ref[0:1], ref[1:2]))

    corner_x, corner_y, corner_z = [pick(ref).astype(jnp.int32) for ref in (sx, sy, sz)]
    strength = tuple(column(jnp.where(core == 0, amplitude[0, k : k + 1], amplitude[1, k : k + 1])) for k in range(2))
    lane = lax.broadcasted_iota(jnp.int32, (16, 128), 1)
    high, low = lane >> 4, lane & 15
    left = below(backward_turn(4 * corner_x * high + corner_y * low)).T
    for p in range(2):
        kz = 2 * me + p
        folded = jnp.where(kz < 128, kz, kz - 256).astype(F32)
        wave_z = 2.0 * math.pi * jnp.full((1, 1), folded, F32) / 256
        shifted = (table[6] + wave_z * wave_z) - centre
        share = (1.0 / (64 * 256 * 256)) / (shifted * shifted + spread * spread)
        value = (shifted * share, spread * share)
        green[p, 0], green[p, 1] = value
        amount = cmul(strength, box_sum(jnp.full((16, 1), kz, jnp.int32)))
        q = cmul(backward_turn(32 * corner_x * high + 16 * corner_y * low + corner_z * kz), amount)
        right = below((beside(q), beside((-q[1], q[0]))))
        sums = jnp.dot(left, right, precision=lax.Precision.HIGHEST, preferred_element_type=F32)
        spectrum[p] = beside(cmul(sides(sums), cmul(value, turns(2))))
    field[...] = jnp.zeros_like(field)
    first[...] = jnp.zeros_like(first)
    loads[0].wait()
    loads[8].wait()
    for x in range(4):
        edge[x : x + 1] = labels[4 * core + x, 0:1]
        edge[4 + x : 5 + x] = labels[4 * core + x, 15:16]
    pl.semaphore_wait(barrier, CHIPS - 1 + 5)

    def to_others(k, source, target, recv_index, device):
        return pltpu.make_async_remote_copy(
            src_ref=source, dst_ref=target, send_sem=edge_send.at[k], recv_sem=edge_recv.at[recv_index],
            device_id=device, device_id_type=MESH,
        )

    def medium_of_cells():
        own = labels.at[pl.ds(4 * core, 4)]
        beside_x = lax.rem(chip_x + 7 + 2 * core, 8)
        copies = [to_others(0, own, own, 0, (sibling, gy))]
        for c in range(2):
            copies.append(
                to_others(1 + c, labels.at[7 * core], near_x.at[1 - core], 2 - core, (2 * beside_x + c, gy))
            )
            for d, to in enumerate((next_y, last_y)):
                copies.append(
                    to_others(3 + 2 * d + c, edge, near_y.at[d, core], 3 + 2 * d + core, (2 * chip_x + c, to))
                )
        for copy in copies:
            copy.start()
        theirs = labels.at[pl.ds(4 - 4 * core, 4)]
        landed = [theirs, near_x.at[0], near_x.at[1]] + [near_y.at[d, c] for d in range(2) for c in range(2)]
        for k, ref in enumerate(landed):
            pltpu.make_async_copy(ref, ref, edge_recv.at[k]).wait()
        for copy in copies:
            copy.wait_send()
        all_labels = labels[...].reshape(128, 256)
        y_low = below((near_y[0, 0, 4:8], near_y[0, 1, 4:8]))
        y_high = below((near_y[1, 0, 0:4], near_y[1, 1, 0:4]))
        for part, (entries, shift) in enumerate(((table_real, centre), (table_imag, spread))):
            values = [look_up(a, entries) for a in (all_labels, near_x[0], near_x[1], y_low, y_high)]
            moved = smoothed(*values) - shift
            potential[part, 0:128] = moved[:, :128].T
            potential[part, 128:256] = moved[:, 128:].T

    def iteration(step, carry):
        for p in range(2):

            @pl.when(step > 0)
            def _():
                arrived(OUT, p)
                v = cmul(halves(matmul(weights(2), split(recv[OUT, p]))), turns(1))
                v = sides(matmul(split(beside(v)), weights(4)))
                spectrum[p] = beside(cmul(v, (green[p, 0], green[p, 1])))
                sent(BACK, p)

            v = cmul_conj(sides(matmul(split(spectrum[p]), weights(5))), turns(1))
            send[BACK, p] = matmul(weights(3), split(below(v)))
            start(BACK, p)

        @pl.when(step == 0)
        def _():
            medium_of_cells()

        arrived(BACK, 0)
        even = halves(matmul(weights(1), split(recv[BACK, 0])))
        arrived(BACK, 1)
        odd = cmul_conj(halves(matmul(weights(1), split(recv[BACK, 1]))), turns(0))
        scattered = [below((even[k] + odd[k], even[k] - odd[k])) for k in range(2)]
        change = [scattered[k] + first[k] - field[k] for k in range(2)]
        moved = cmul((potential[0], potential[1]), change)
        field[0], field[1] = field[0] - moved[1] * inverse, field[1] + moved[0] * inverse

        @pl.when(step == 0)
        def _():
            first[0], first[1] = scattered

        @pl.when(step < ITERS - 1)
        def _():
            v = cmul((potential[0], potential[1]), (field[0], field[1]))
            upper, lower = halves(v[0]), halves(v[1])
            inputs = (
                (upper[0] + upper[1], lower[0] + lower[1]),
                cmul((upper[0] - upper[1], lower[0] - lower[1]), turns(0)),
            )
            for p in range(2):

                @pl.when(step > 0)
                def _():
                    sent(OUT, p)

                send[OUT, p] = matmul(weights(0), split(below(inputs[p])))
                start(OUT, p)

        return carry

    lax.fori_loop(0, ITERS, iteration, 0)

    for part in range(2):
        result[part] = beside((field[part, 0:128].T, field[part, 128:256].T)).reshape(8, 16, 256)
    theirs = pltpu.make_async_remote_copy(
        src_ref=result.at[:, pl.ds(4 - 4 * core, 4)], dst_ref=out.at[core], send_sem=half_send, recv_sem=half_recv,
        device_id=(sibling, gy), device_id_type=MESH,
    )
    theirs.start()
    out[core] = result[:, pl.ds(4 * core, 4)]
    landed = out.at[1 - core]
    pltpu.make_async_copy(landed, landed, half_recv).wait()
    theirs.wait_send()
    for stage in range(2):
        for p in range(2):
            sent(stage, p)


def per_device(labels, speed, absorption, amplitude, source_x, source_y, source_z):
    anywhere = pl.BlockSpec(memory_space=pl.ANY)
    dma = pltpu.SemaphoreType.DMA
    return pl.pallas_call(
        kernel,
        out_shape=jax.ShapeDtypeStruct((2, 2, 4, 16, 256), F32),
        in_specs=[anywhere] * 9,
        out_specs=pl.BlockSpec(memory_space=pltpu.VMEM),
        scratch_shapes=[
            pltpu.VMEM((1, 8), F32),
            pltpu.VMEM((1, 8), F32),
            pltpu.VMEM((2, 2, 16), F32),
            pltpu.VMEM((2, 16), jnp.int32),
            pltpu.VMEM((2, 16), jnp.int32),
            pltpu.VMEM((2, 16), jnp.int32),
            pltpu.VMEM((12, 256, 256), BF16),
            pltpu.VMEM((7, 128, 128), F32),
            pltpu.VMEM((8, 16, 256), jnp.int32),
            pltpu.VMEM((2, 16, 256), jnp.int32),
            pltpu.VMEM((2, 2, 8, 256), jnp.int32),
            pltpu.VMEM((8, 256), jnp.int32),
            pltpu.VMEM((2, 256, 128), F32),
            pltpu.VMEM((2, 256, 128), F32),
            pltpu.VMEM((2, 256, 128), F32),
            pltpu.VMEM((2, 2, 128, 128), F32),
            pltpu.VMEM((2, 128, 256), F32),
            pltpu.VMEM((2, 8, 16, 256), F32),
            pltpu.VMEM((2, 2, 2 * CHIPS, 128), F32),
            pltpu.VMEM((2, 2, 2 * CHIPS, 128), F32),
            dma((9,)),
            dma((2, 2)),
            dma((2, 2)),
            dma((7,)),
            dma((7,)),
            dma,
            dma,
        ],
        compiler_params=pltpu.CompilerParams(
            collective_id=0, has_side_effects=True, vmem_limit_bytes=56 * 1024 * 1024
        ),
    )(
        labels,
        speed.reshape(1, 8),
        absorption.reshape(1, 8),
        jnp.transpose(amplitude, (0, 2, 1)),
        source_x,
        source_y,
        source_z,
        jnp.asarray(transform_matrices()),
        jnp.asarray(constant_tables()),
    )


def solution(mesh):
    return jax.shard_map(
        per_device,
        mesh=mesh,
        in_specs=(P("gx", "gy", None), P(), P(), P(), P(), P(), P()),
        out_specs=P(None, None, "gx", "gy", None),
        check_vma=False,
    )
```

```python
import functools
import math

import jax
import jax.numpy as jnp
import numpy as np
from jax import lax
from jax.experimental import pallas as pl
from jax.experimental.pallas import tpu as pltpu
from jax.sharding import PartitionSpec as P

ITERS = 4
CHIPS = 128
MESH = pl.DeviceIdType.MESH
F32 = jnp.float32
BF16 = jnp.bfloat16
WAVE = 2.0 * math.pi / 6.0
OUT, BACK = range(2)


def transform_matrices():
    def both(phase):
        c, s = np.cos(2.0 * np.pi * phase), np.sin(2.0 * np.pi * phase)
        return np.block([[c, s], [-s, c]]), np.block([[c, -s], [s, c]])

    n = np.arange(128)
    pairs = (np.arange(2)[None, :] * 128 + n[:, None]).reshape(-1)
    z_out, z_back = both((np.outer(n, n) % 128) / 128)
    high, low = n >> 4, n & 15
    mixed = ((2 * np.outer(high, high) + np.outer(low, low)) % 16) / 16
    far_out, far_back = both(mixed)
    near_back, near_out = both(mixed)
    parts = []
    for matrix in (z_out[pairs], z_back[:, pairs], far_out[:, pairs], far_back[pairs], near_out, near_back):
        high = matrix.astype(BF16)
        parts.append(high)
        parts.append((matrix - high.astype(np.float64)).astype(BF16))
    return np.stack(parts)


def constant_tables():
    n = np.arange(128)
    row, lane = n[:, None], n[None, :]
    z_turn = np.exp(-2j * np.pi * row / 256) * np.ones((1, 128))
    xy_turn = np.exp(-2j * np.pi * ((row >> 4) * (lane >> 4) / 64 + (row & 15) * (lane & 15) / 256))
    kx, ky = (row >> 4) + 8 * (lane >> 4), (row & 15) + 16 * (lane & 15)
    box = sum(np.exp(-2j * np.pi * j * kx / 64) for j in range(4)) * sum(np.exp(-2j * np.pi * j * ky / 256) for j in range(4))
    wave = [
        (2.0 * np.pi * np.where(k < size // 2, k, k - size) / size).astype(np.float32) for k, size in ((kx, 64), (ky, 256))
    ]
    tables = [z_turn.real, z_turn.imag, xy_turn.real, xy_turn.imag, box.real, box.imag]
    return np.stack([t.astype(np.float32) for t in tables] + [wave[0] * wave[0] + wave[1] * wave[1]])


def cos_turn(m):
    m = m & 255
    t = (64 - jnp.minimum(m, 256 - m)).astype(F32) * (2.0 * math.pi / 256)
    q = t * t
    poly = -1.0 / 39916800
    for term in (1.0 / 362880, -1.0 / 5040, 1.0 / 120, -1.0 / 6, 1.0):
        poly = poly * q + term
    return t * poly


def backward_turn(m):
    return cos_turn(m), -cos_turn(m - 64)


def cmul(a, b):
    return a[0] * b[0] - a[1] * b[1], a[0] * b[1] + a[1] * b[0]


def cmul_conj(a, b):
    return a[0] * b[0] + a[1] * b[1], a[1] * b[0] - a[0] * b[1]


def box_sum(m):
    w = backward_turn(m)
    square = backward_turn(2 * m)
    return cmul((1.0 + w[0], w[1]), (1.0 + square[0], square[1]))


def split(x):
    high = x.astype(BF16)
    return high, (x - high.astype(F32)).astype(BF16)


def matmul(a, b):
    dot = functools.partial(jnp.dot, preferred_element_type=F32)
    return dot(a[0], b[0]) + (dot(a[0], b[1]) + dot(a[1], b[0]))


def medium(speed, absorption):
    k = WAVE / speed
    real = k * k - absorption * absorption
    imag = 2.0 * k * absorption
    centre = 0.5 * (jnp.min(real, axis=1, keepdims=True) + jnp.max(real, axis=1, keepdims=True))
    size = jnp.sqrt((real - centre) ** 2 + imag * imag)
    return real, imag, centre, 1.05 * jnp.max(size, axis=1, keepdims=True)


def look_up(labels, table):
    out = jnp.broadcast_to(table[:, 0:1], labels.shape)
    for l in range(1, table.shape[1]):
        out = jnp.where(labels == l, table[:, l : l + 1], out)
    return out


def column(row):
    n = row.shape[1]
    eye = lax.broadcasted_iota(jnp.int32, (n, n), 0) == lax.broadcasted_iota(jnp.int32, (n, n), 1)
    spread_out = jnp.where(eye, jnp.broadcast_to(row.astype(F32), (n, n)), 0.0)
    return jnp.sum(spread_out, axis=1, keepdims=True)


def smoothed(own, x_low, x_high, y_low, y_high):
    row = lax.broadcasted_iota(jnp.int32, own.shape, 0) & 15

    def per_x(edge):
        return jnp.concatenate([jnp.broadcast_to(edge[x : x + 1], (16, 256)) for x in range(8)], axis=0)

    total = jnp.concatenate([x_low, own[:112]], axis=0) + jnp.concatenate([own[16:], x_high], axis=0)
    total = total + jnp.where(row == 0, per_x(y_low), pltpu.roll(own, 1, 0))
    total = total + jnp.where(row == 15, per_x(y_high), pltpu.roll(own, 127, 0))
    total = total + pltpu.roll(own, 1, 1) + pltpu.roll(own, 255, 1)
    return 0.5 * own + total * (1.0 / 12.0)


def farthest_first():
    offsets = [(y, x, z) for y in range(4) for x in range(4) for z in range(8)][1:]

    def hops(step, size):
        return min(step, size - step)

    return sorted(offsets, key=lambda o: (-(hops(o[0], 4) + hops(o[1], 4) + hops(o[2], 8)), hops(o[2], 8)))


def kernel(
    labels_hbm, speed_hbm, absorption_hbm, amplitude_hbm, sx_hbm, sy_hbm, sz_hbm, matrix_hbm, table_hbm, out,
    speed, absorption, amplitude, sx, sy, sz, matrix, table,
    labels, near_x, near_y, edge, potential, field, first, green, spectrum, result, send, recv,
    load_sem, send_sem, recv_sem, edge_send, edge_recv, half_send, half_recv,
):
    gx, gy = lax.axis_index("gx"), lax.axis_index("gy")
    core, chip_x = lax.rem(gx, 2), gx // 2
    me = chip_x * 16 + gy
    sibling = chip_x * 2 + 1 - core
    next_x, last_x = lax.rem(chip_x + 1, 8), lax.rem(chip_x + 7, 8)
    next_y, last_y = lax.rem(gy + 1, 16), lax.rem(gy + 15, 16)

    loads = [
        pltpu.make_async_copy(source, target, load_sem.at[k])
        for k, (source, target) in enumerate(
            (
                (labels_hbm, labels.at[pl.ds(4 * core, 4)]),
                (speed_hbm, speed),
                (absorption_hbm, absorption),
                (amplitude_hbm, amplitude),
                (sx_hbm, sx),
                (sy_hbm, sy),
                (sz_hbm, sz),
                (table_hbm, table),
                (matrix_hbm, matrix),
            )
        )
    ]
    for load in loads:
        load.start()

    place_y, place_x, place_z = 2 * (gy // 8) + gx // 8, lax.rem(chip_x, 4), lax.rem(gy, 8)
    ys = [lax.rem(place_y + d, 4) for d in range(4)]
    xs = [lax.rem(place_x + d, 4) for d in range(4)]
    zs = [lax.rem(place_z + d, 8) for d in range(8)]
    to_x = [[lax.rem(y, 2) * 4 + x for x in xs] for y in ys]
    to_y = [[(y // 2) * 8 + z for z in zs] for y in ys]
    order = farthest_first()

    barrier = pltpu.get_barrier_semaphore()

    def greet(device):
        pl.semaphore_signal(barrier, inc=1, device_id=device, device_id_type=MESH)

    for y, x, z in order:
        greet((2 * to_x[y][x] + core, to_y[y][z]))
    greet((sibling, gy))
    greet((2 * next_x + 1 - core, gy))
    greet((2 * last_x + 1 - core, gy))
    greet((sibling, next_y))
    greet((sibling, last_y))

    def start(stage, p):
        target = recv.at[stage, p, pl.ds(2 * me, 2)]
        for y, x, z in order:
            pltpu.make_async_remote_copy(
                src_ref=send.at[stage, p, pl.ds(2 * (to_x[y][x] * 16 + to_y[y][z]), 2)],
                dst_ref=target,
                send_sem=send_sem.at[stage, p],
                recv_sem=recv_sem.at[stage, p],
                device_id=(2 * to_x[y][x] + core, to_y[y][z]),
                device_id_type=MESH,
            ).start()
        pltpu.make_async_copy(send.at[stage, p, pl.ds(2 * me, 2)], target, recv_sem.at[stage, p]).start()

    def arrived(stage, p):
        whole = recv.at[stage, p]
        pltpu.make_async_copy(whole, whole, recv_sem.at[stage, p]).wait()

    def sent(stage, p):
        part = send.at[stage, p, pl.ds(0, 2 * CHIPS - 2)]
        pltpu.make_async_copy(part, part, send_sem.at[stage, p]).wait()

    def weights(k):
        return matrix[2 * k], matrix[2 * k + 1]

    def turns(k):
        return table[2 * k], table[2 * k + 1]

    def halves(a):
        return a[:128], a[128:]

    def sides(a):
        return a[:, :128], a[:, 128:]

    def beside(v):
        return jnp.concatenate(v, axis=1)

    def below(v):
        return jnp.concatenate(v, axis=0)

    def to_space(v):
        v = cmul_conj(sides(matmul(split(beside(v)), weights(5))), turns(1))
        return matmul(weights(3), split(below(v)))

    for load in loads[1:8]:
        load.wait()
    table_real, table_imag, centre, spread = medium(speed[...], absorption[...])
    inverse = 1.0 / spread

    def pick(ref):
        return column(jnp.where(core == 0, ref[0:1], ref[1:2]))

    corner_x, corner_y, corner_z = [pick(ref).astype(jnp.int32) for ref in (sx, sy, sz)]
    strength = tuple(column(jnp.where(core == 0, amplitude[0, k : k + 1], amplitude[1, k : k + 1])) for k in range(2))
    lane = lax.broadcasted_iota(jnp.int32, (16, 128), 1)
    high, low = lane >> 4, lane & 15
    left = below(backward_turn(4 * corner_x * high + corner_y * low)).T
    for p in range(2):
        kz = 2 * me + p
        folded = jnp.where(kz < 128, kz, kz - 256).astype(F32)
        wave_z = 2.0 * math.pi * jnp.full((1, 1), folded, F32) / 256
        shifted = (table[6] + wave_z * wave_z) - centre
        share = (1.0 / (64 * 256 * 256)) / (shifted * shifted + spread * spread)
        value = (shifted * share, spread * share)
        green[p, 0], green[p, 1] = value
        amount = cmul(strength, box_sum(jnp.full((16, 1), kz, jnp.int32)))
        q = cmul(backward_turn(32 * corner_x * high + 16 * corner_y * low + corner_z * kz), amount)
        right = below((beside(q), beside((-q[1], q[0]))))
        sums = jnp.dot(left, right, precision=lax.Precision.HIGHEST, preferred_element_type=F32)
        spectrum[p] = beside(cmul(sides(sums), cmul(value, turns(2))))
    field[...] = jnp.zeros_like(field)
    first[...] = jnp.zeros_like(first)
    loads[0].wait()
    loads[8].wait()
    for p in range(2):
        send[BACK, p] = to_space(sides(spectrum[p]))
    for x in range(4):
        edge[x : x + 1] = labels[4 * core + x, 0:1]
        edge[4 + x : 5 + x] = labels[4 * core + x, 15:16]
    pl.semaphore_wait(barrier, CHIPS - 1 + 5)

    def to_others(k, source, target, recv_index, device):
        return pltpu.make_async_remote_copy(
            src_ref=source, dst_ref=target, send_sem=edge_send.at[k], recv_sem=edge_recv.at[recv_index],
            device_id=device, device_id_type=MESH,
        )

    def medium_of_cells():
        own = labels.at[pl.ds(4 * core, 4)]
        beside_x = lax.rem(chip_x + 7 + 2 * core, 8)
        copies = [to_others(0, own, own, 0, (sibling, gy))]
        for c in range(2):
            copies.append(
                to_others(1 + c, labels.at[7 * core], near_x.at[1 - core], 2 - core, (2 * beside_x + c, gy))
            )
            for d, to in enumerate((next_y, last_y)):
                copies.append(
                    to_others(3 + 2 * d + c, edge, near_y.at[d, core], 3 + 2 * d + core, (2 * chip_x + c, to))
                )
        for copy in copies:
            copy.start()
        theirs = labels.at[pl.ds(4 - 4 * core, 4)]
        landed = [theirs, near_x.at[0], near_x.at[1]] + [near_y.at[d, c] for d in range(2) for c in range(2)]
        for k, ref in enumerate(landed):
            pltpu.make_async_copy(ref, ref, edge_recv.at[k]).wait()
        for copy in copies:
            copy.wait_send()
        all_labels = labels[...].reshape(128, 256)
        y_low = below((near_y[0, 0, 4:8], near_y[0, 1, 4:8]))
        y_high = below((near_y[1, 0, 0:4], near_y[1, 1, 0:4]))
        for part, (entries, shift) in enumerate(((table_real, centre), (table_imag, spread))):
            values = [look_up(a, entries) for a in (all_labels, near_x[0], near_x[1], y_low, y_high)]
            moved = smoothed(*values) - shift
            potential[part, 0:128] = moved[:, :128].T
            potential[part, 128:256] = moved[:, 128:].T

    def iteration(step, carry):
        for p in range(2):

            @pl.when(step > 0)
            def _():
                arrived(OUT, p)
                v = cmul(halves(matmul(weights(2), split(recv[OUT, p]))), turns(1))
                v = sides(matmul(split(beside(v)), weights(4)))
                v = to_space(cmul(v, (green[p, 0], green[p, 1])))
                sent(BACK, p)
                send[BACK, p] = v

            start(BACK, p)

        @pl.when(step == 0)
        def _():
            medium_of_cells()

        arrived(BACK, 0)
        even = halves(matmul(weights(1), split(recv[BACK, 0])))
        arrived(BACK, 1)
        odd = cmul_conj(halves(matmul(weights(1), split(recv[BACK, 1]))), turns(0))
        scattered = [below((even[k] + odd[k], even[k] - odd[k])) for k in range(2)]
        change = [scattered[k] + first[k] - field[k] for k in range(2)]
        moved = cmul((potential[0], potential[1]), change)
        field[0], field[1] = field[0] - moved[1] * inverse, field[1] + moved[0] * inverse

        @pl.when(step == 0)
        def _():
            first[0], first[1] = scattered

        @pl.when(step < ITERS - 1)
        def _():
            v = cmul((potential[0], potential[1]), (field[0], field[1]))
            upper, lower = halves(v[0]), halves(v[1])
            inputs = (
                (upper[0] + upper[1], lower[0] + lower[1]),
                cmul((upper[0] - upper[1], lower[0] - lower[1]), turns(0)),
            )
            for p in range(2):

                @pl.when(step > 0)
                def _():
                    sent(OUT, p)

                send[OUT, p] = matmul(weights(0), split(below(inputs[p])))
                start(OUT, p)

        return carry

    lax.fori_loop(0, ITERS, iteration, 0)

    for part in range(2):
        result[part] = beside((field[part, 0:128].T, field[part, 128:256].T)).reshape(8, 16, 256)
    theirs = pltpu.make_async_remote_copy(
        src_ref=result.at[:, pl.ds(4 - 4 * core, 4)], dst_ref=out.at[core], send_sem=half_send, recv_sem=half_recv,
        device_id=(sibling, gy), device_id_type=MESH,
    )
    theirs.start()
    out[core] = result[:, pl.ds(4 * core, 4)]
    landed = out.at[1 - core]
    pltpu.make_async_copy(landed, landed, half_recv).wait()
    theirs.wait_send()
    for stage in range(2):
        for p in range(2):
            sent(stage, p)


def per_device(labels, speed, absorption, amplitude, source_x, source_y, source_z):
    anywhere = pl.BlockSpec(memory_space=pl.ANY)
    dma = pltpu.SemaphoreType.DMA
    return pl.pallas_call(
        kernel,
        out_shape=jax.ShapeDtypeStruct((2, 2, 4, 16, 256), F32),
        in_specs=[anywhere] * 9,
        out_specs=pl.BlockSpec(memory_space=pltpu.VMEM),
        scratch_shapes=[
            pltpu.VMEM((1, 8), F32),
            pltpu.VMEM((1, 8), F32),
            pltpu.VMEM((2, 2, 16), F32),
            pltpu.VMEM((2, 16), jnp.int32),
            pltpu.VMEM((2, 16), jnp.int32),
            pltpu.VMEM((2, 16), jnp.int32),
            pltpu.VMEM((12, 256, 256), BF16),
            pltpu.VMEM((7, 128, 128), F32),
            pltpu.VMEM((8, 16, 256), jnp.int32),
            pltpu.VMEM((2, 16, 256), jnp.int32),
            pltpu.VMEM((2, 2, 8, 256), jnp.int32),
            pltpu.VMEM((8, 256), jnp.int32),
            pltpu.VMEM((2, 256, 128), F32),
            pltpu.VMEM((2, 256, 128), F32),
            pltpu.VMEM((2, 256, 128), F32),
            pltpu.VMEM((2, 2, 128, 128), F32),
            pltpu.VMEM((2, 128, 256), F32),
            pltpu.VMEM((2, 8, 16, 256), F32),
            pltpu.VMEM((2, 2, 2 * CHIPS, 128), F32),
            pltpu.VMEM((2, 2, 2 * CHIPS, 128), F32),
            dma((9,)),
            dma((2, 2)),
            dma((2, 2)),
            dma((7,)),
            dma((7,)),
            dma,
            dma,
        ],
        compiler_params=pltpu.CompilerParams(
            collective_id=0, has_side_effects=True, vmem_limit_bytes=32 * 1024 * 1024
        ),
    )(*(pltpu.with_memory_space_constraint(a, pltpu.HBM) for a in (
        labels,
        speed.reshape(1, 8),
        absorption.reshape(1, 8),
        jnp.transpose(amplitude, (0, 2, 1)),
        source_x,
        source_y,
        source_z,
        jnp.asarray(transform_matrices()),
        jnp.asarray(constant_tables()),
    )))


def solution(mesh):
    return jax.shard_map(
        per_device,
        mesh=mesh,
        in_specs=(P("gx", "gy", None), P(), P(), P(), P(), P(), P()),
        out_specs=P(None, None, "gx", "gy", None),
        check_vma=False,
    )
```

```python
import functools
import math

import jax
import jax.numpy as jnp
import numpy as np
from jax import lax
from jax.experimental import pallas as pl
from jax.experimental.pallas import tpu as pltpu
from jax.sharding import PartitionSpec as P

ITERS = 4
CHIPS = 128
MESH = pl.DeviceIdType.MESH
F32 = jnp.float32
BF16 = jnp.bfloat16
WAVE = 2.0 * math.pi / 6.0
OUT, BACK = range(2)


def transform_matrices():
    def both(phase):
        c, s = np.cos(2.0 * np.pi * phase), np.sin(2.0 * np.pi * phase)
        return np.block([[c, s], [-s, c]]), np.block([[c, -s], [s, c]])

    n = np.arange(128)
    pairs = (np.arange(2)[None, :] * 128 + n[:, None]).reshape(-1)
    z_out, z_back = both((np.outer(n, n) % 128) / 128)
    high, low = n >> 4, n & 15
    mixed = ((2 * np.outer(high, high) + np.outer(low, low)) % 16) / 16
    far_out, far_back = both(mixed)
    near_back, near_out = both(mixed)
    parts = []
    for matrix in (z_out[pairs], z_back[:, pairs], far_out[:, pairs], far_back[pairs], near_out, near_back):
        high = matrix.astype(BF16)
        parts.append(high)
        parts.append((matrix - high.astype(np.float64)).astype(BF16))
    return np.stack(parts)


def constant_tables():
    n = np.arange(128)
    row, lane = n[:, None], n[None, :]
    z_turn = np.exp(-2j * np.pi * row / 256) * np.ones((1, 128))
    xy_turn = np.exp(-2j * np.pi * ((row >> 4) * (lane >> 4) / 64 + (row & 15) * (lane & 15) / 256))
    kx, ky = (row >> 4) + 8 * (lane >> 4), (row & 15) + 16 * (lane & 15)
    box = sum(np.exp(-2j * np.pi * j * kx / 64) for j in range(4)) * sum(np.exp(-2j * np.pi * j * ky / 256) for j in range(4))
    wave = [
        (2.0 * np.pi * np.where(k < size // 2, k, k - size) / size).astype(np.float32) for k, size in ((kx, 64), (ky, 256))
    ]
    tables = [z_turn.real, z_turn.imag, xy_turn.real, xy_turn.imag, box.real, box.imag]
    return np.stack([t.astype(np.float32) for t in tables] + [wave[0] * wave[0] + wave[1] * wave[1]])


def cos_turn(m):
    m = m & 255
    t = (64 - jnp.minimum(m, 256 - m)).astype(F32) * (2.0 * math.pi / 256)
    q = t * t
    poly = -1.0 / 39916800
    for term in (1.0 / 362880, -1.0 / 5040, 1.0 / 120, -1.0 / 6, 1.0):
        poly = poly * q + term
    return t * poly


def backward_turn(m):
    return cos_turn(m), -cos_turn(m - 64)


def cmul(a, b):
    return a[0] * b[0] - a[1] * b[1], a[0] * b[1] + a[1] * b[0]


def cmul_conj(a, b):
    return a[0] * b[0] + a[1] * b[1], a[1] * b[0] - a[0] * b[1]


def box_sum(m):
    w = backward_turn(m)
    square = backward_turn(2 * m)
    return cmul((1.0 + w[0], w[1]), (1.0 + square[0], square[1]))


def split(x):
    high = x.astype(BF16)
    return high, (x - high.astype(F32)).astype(BF16)


def matmul(a, b):
    dot = functools.partial(jnp.dot, preferred_element_type=F32)
    return dot(a[0], b[0]) + (dot(a[0], b[1]) + dot(a[1], b[0]))


def medium(speed, absorption):
    k = WAVE / speed
    real = k * k - absorption * absorption
    imag = 2.0 * k * absorption
    centre = 0.5 * (jnp.min(real, axis=1, keepdims=True) + jnp.max(real, axis=1, keepdims=True))
    size = jnp.sqrt((real - centre) ** 2 + imag * imag)
    return real, imag, centre, 1.05 * jnp.max(size, axis=1, keepdims=True)


def look_up(labels, table):
    out = jnp.broadcast_to(table[:, 0:1], labels.shape)
    for l in range(1, table.shape[1]):
        out = jnp.where(labels == l, table[:, l : l + 1], out)
    return out


def column(row):
    n = row.shape[1]
    eye = lax.broadcasted_iota(jnp.int32, (n, n), 0) == lax.broadcasted_iota(jnp.int32, (n, n), 1)
    spread_out = jnp.where(eye, jnp.broadcast_to(row.astype(F32), (n, n)), 0.0)
    return jnp.sum(spread_out, axis=1, keepdims=True)


def smoothed(own, x_low, x_high, y_low, y_high):
    row = lax.broadcasted_iota(jnp.int32, own.shape, 0) & 15

    def per_x(edge):
        return jnp.concatenate([jnp.broadcast_to(edge[x : x + 1], (16, 256)) for x in range(8)], axis=0)

    total = jnp.concatenate([x_low, own[:112]], axis=0) + jnp.concatenate([own[16:], x_high], axis=0)
    total = total + jnp.where(row == 0, per_x(y_low), pltpu.roll(own, 1, 0))
    total = total + jnp.where(row == 15, per_x(y_high), pltpu.roll(own, 127, 0))
    total = total + pltpu.roll(own, 1, 1) + pltpu.roll(own, 255, 1)
    return 0.5 * own + total * (1.0 / 12.0)


def farthest_first():
    offsets = [(y, x, z) for y in range(4) for x in range(4) for z in range(8)][1:]

    def hops(step, size):
        return min(step, size - step)

    return sorted(offsets, key=lambda o: (-(hops(o[0], 4) + hops(o[1], 4) + hops(o[2], 8)), hops(o[2], 8)))


def kernel(
    labels_hbm, speed_hbm, absorption_hbm, amplitude_hbm, sx_hbm, sy_hbm, sz_hbm, matrix_hbm, table_hbm, out,
    speed, absorption, amplitude, sx, sy, sz, matrix, table,
    labels, near_x, near_y, edge, potential, field, first, green, spectrum, result, send, recv,
    load_sem, send_sem, recv_sem, edge_send, edge_recv, half_send, half_recv,
):
    gx, gy = lax.axis_index("gx"), lax.axis_index("gy")
    core, chip_x = lax.rem(gx, 2), gx // 2
    me = chip_x * 16 + gy
    sibling = chip_x * 2 + 1 - core
    next_x, last_x = lax.rem(chip_x + 1, 8), lax.rem(chip_x + 7, 8)
    next_y, last_y = lax.rem(gy + 1, 16), lax.rem(gy + 15, 16)

    loads = [
        pltpu.make_async_copy(source, target, load_sem.at[k])
        for k, (source, target) in enumerate(
            (
                (labels_hbm, labels.at[pl.ds(4 * core, 4)]),
                (speed_hbm, speed),
                (absorption_hbm, absorption),
                (amplitude_hbm, amplitude),
                (sx_hbm, sx),
                (sy_hbm, sy),
                (sz_hbm, sz),
                (table_hbm, table),
                (matrix_hbm, matrix),
            )
        )
    ]
    for load in loads:
        load.start()

    place_y, place_x, place_z = 2 * (gy // 8) + gx // 8, lax.rem(chip_x, 4), lax.rem(gy, 8)
    ys = [lax.rem(place_y + d, 4) for d in range(4)]
    xs = [lax.rem(place_x + d, 4) for d in range(4)]
    zs = [lax.rem(place_z + d, 8) for d in range(8)]
    to_x = [[lax.rem(y, 2) * 4 + x for x in xs] for y in ys]
    to_y = [[(y // 2) * 8 + z for z in zs] for y in ys]
    order = farthest_first()

    barrier = pltpu.get_barrier_semaphore()

    def greet(device):
        pl.semaphore_signal(barrier, inc=1, device_id=device, device_id_type=MESH)

    for y, x, z in order:
        greet((2 * to_x[y][x] + core, to_y[y][z]))
    greet((sibling, gy))
    greet((2 * next_x + 1 - core, gy))
    greet((2 * last_x + 1 - core, gy))
    greet((sibling, next_y))
    greet((sibling, last_y))

    def start(stage, p):
        target = recv.at[stage, p, pl.ds(2 * me, 2)]
        for y, x, z in order:
            pltpu.make_async_remote_copy(
                src_ref=send.at[stage, p, pl.ds(2 * (to_x[y][x] * 16 + to_y[y][z]), 2)],
                dst_ref=target,
                send_sem=send_sem.at[stage, p],
                recv_sem=recv_sem.at[stage, p],
                device_id=(2 * to_x[y][x] + core, to_y[y][z]),
                device_id_type=MESH,
            ).start()
        pltpu.make_async_copy(send.at[stage, p, pl.ds(2 * me, 2)], target, recv_sem.at[stage, p]).start()

    def arrived(stage, p):
        whole = recv.at[stage, p]
        pltpu.make_async_copy(whole, whole, recv_sem.at[stage, p]).wait()

    def sent(stage, p):
        part = send.at[stage, p, pl.ds(0, 2 * CHIPS - 2)]
        pltpu.make_async_copy(part, part, send_sem.at[stage, p]).wait()

    def weights(k):
        return matrix[2 * k], matrix[2 * k + 1]

    def turns(k):
        return table[2 * k], table[2 * k + 1]

    def halves(a):
        return a[:128], a[128:]

    def sides(a):
        return a[:, :128], a[:, 128:]

    def beside(v):
        return jnp.concatenate(v, axis=1)

    def below(v):
        return jnp.concatenate(v, axis=0)

    def to_space(v):
        v = cmul_conj(sides(matmul(split(beside(v)), weights(5))), turns(1))
        return matmul(weights(3), split(below(v)))

    for load in loads[1:8]:
        load.wait()
    table_real, table_imag, centre, spread = medium(speed[...], absorption[...])
    inverse = 1.0 / spread

    def pick(ref):
        return column(jnp.where(core == 0, ref[0:1], ref[1:2]))

    corner_x, corner_y, corner_z = [pick(ref).astype(jnp.int32) for ref in (sx, sy, sz)]
    strength = tuple(column(jnp.where(core == 0, amplitude[0, k : k + 1], amplitude[1, k : k + 1])) for k in range(2))
    lane = lax.broadcasted_iota(jnp.int32, (16, 128), 1)
    high, low = lane >> 4, lane & 15
    left = below(backward_turn(4 * corner_x * high + corner_y * low)).T
    for p in range(2):
        kz = 2 * me + p
        folded = jnp.where(kz < 128, kz, kz - 256).astype(F32)
        wave_z = 2.0 * math.pi * jnp.full((1, 1), folded, F32) / 256
        shifted = (table[6] + wave_z * wave_z) - centre
        share = (1.0 / (64 * 256 * 256)) / (shifted * shifted + spread * spread)
        value = (shifted * share, spread * share)
        green[p, 0], green[p, 1] = value
        amount = cmul(strength, box_sum(jnp.full((16, 1), kz, jnp.int32)))
        q = cmul(backward_turn(32 * corner_x * high + 16 * corner_y * low + corner_z * kz), amount)
        right = below((beside(q), beside((-q[1], q[0]))))
        sums = jnp.dot(left, right, precision=lax.Precision.HIGHEST, preferred_element_type=F32)
        spectrum[p] = beside(cmul(sides(sums), cmul(value, turns(2))))
    field[...] = jnp.zeros_like(field)
    first[...] = jnp.zeros_like(first)
    loads[0].wait()
    loads[8].wait()
    for p in range(2):
        send[BACK, p] = to_space(sides(spectrum[p]))
    for x in range(4):
        edge[x : x + 1] = labels[4 * core + x, 0:1]
        edge[4 + x : 5 + x] = labels[4 * core + x, 15:16]
    pl.semaphore_wait(barrier, CHIPS - 1 + 5)

    def to_others(k, source, target, recv_index, device):
        return pltpu.make_async_remote_copy(
            src_ref=source, dst_ref=target, send_sem=edge_send.at[k], recv_sem=edge_recv.at[recv_index],
            device_id=device, device_id_type=MESH,
        )

    own = labels.at[pl.ds(4 * core, 4)]
    beside_x = lax.rem(chip_x + 7 + 2 * core, 8)
    copies = [to_others(0, own, own, 0, (sibling, gy))]
    for c in range(2):
        copies.append(
            to_others(1 + c, labels.at[7 * core], near_x.at[1 - core], 2 - core, (2 * beside_x + c, gy))
        )
        for d, to in enumerate((next_y, last_y)):
            copies.append(
                to_others(3 + 2 * d + c, edge, near_y.at[d, core], 3 + 2 * d + core, (2 * chip_x + c, to))
            )

    def medium_of_cells():
        theirs = labels.at[pl.ds(4 - 4 * core, 4)]
        landed = [theirs, near_x.at[0], near_x.at[1]] + [near_y.at[d, c] for d in range(2) for c in range(2)]
        for k, ref in enumerate(landed):
            pltpu.make_async_copy(ref, ref, edge_recv.at[k]).wait()
        for copy in copies:
            copy.wait_send()
        all_labels = labels[...].reshape(128, 256)
        y_low = below((near_y[0, 0, 4:8], near_y[0, 1, 4:8]))
        y_high = below((near_y[1, 0, 0:4], near_y[1, 1, 0:4]))
        for part, (entries, shift) in enumerate(((table_real, centre), (table_imag, spread))):
            values = [look_up(a, entries) for a in (all_labels, near_x[0], near_x[1], y_low, y_high)]
            moved = smoothed(*values) - shift
            potential[part, 0:128] = moved[:, :128].T
            potential[part, 128:256] = moved[:, 128:].T

    def iteration(step, carry):
        for p in range(2):

            @pl.when(step > 0)
            def _():
                arrived(OUT, p)
                v = cmul(halves(matmul(weights(2), split(recv[OUT, p]))), turns(1))
                v = sides(matmul(split(beside(v)), weights(4)))
                v = to_space(cmul(v, (green[p, 0], green[p, 1])))
                sent(BACK, p)
                send[BACK, p] = v

            start(BACK, p)
            if p == 0:

                @pl.when(step == 0)
                def _():
                    for copy in copies:
                        copy.start()


        @pl.when(step == 0)
        def _():
            medium_of_cells()

        arrived(BACK, 0)
        even = halves(matmul(weights(1), split(recv[BACK, 0])))
        arrived(BACK, 1)
        odd = cmul_conj(halves(matmul(weights(1), split(recv[BACK, 1]))), turns(0))
        scattered = [below((even[k] + odd[k], even[k] - odd[k])) for k in range(2)]
        change = [scattered[k] + first[k] - field[k] for k in range(2)]
        moved = cmul((potential[0], potential[1]), change)
        field[0], field[1] = field[0] - moved[1] * inverse, field[1] + moved[0] * inverse

        @pl.when(step == 0)
        def _():
            first[0], first[1] = scattered

        @pl.when(step < ITERS - 1)
        def _():
            v = cmul((potential[0], potential[1]), (field[0], field[1]))
            upper, lower = halves(v[0]), halves(v[1])
            inputs = (
                (upper[0] + upper[1], lower[0] + lower[1]),
                cmul((upper[0] - upper[1], lower[0] - lower[1]), turns(0)),
            )
            for p in range(2):

                @pl.when(step > 0)
                def _():
                    sent(OUT, p)

                send[OUT, p] = matmul(weights(0), split(below(inputs[p])))
                start(OUT, p)

        return carry

    lax.fori_loop(0, ITERS, iteration, 0)

    copies = []
    for part in range(2):
        result[part] = beside((field[part, 0:128].T, field[part, 128:256].T)).reshape(8, 16, 256)
        copies.append(
            pltpu.make_async_remote_copy(
                src_ref=result.at[part, pl.ds(4 - 4 * core, 4)], dst_ref=out.at[core, part],
                send_sem=half_send.at[part], recv_sem=half_recv.at[part],
                device_id=(sibling, gy), device_id_type=MESH,
            )
        )
        copies[part].start()
    for part in range(2):
        out[core, part] = result[part, pl.ds(4 * core, 4)]
    for stage in range(2):
        for p in range(2):
            sent(stage, p)
    for part in range(2):
        landed = out.at[1 - core, part]
        pltpu.make_async_copy(landed, landed, half_recv.at[part]).wait()
        copies[part].wait_send()


def per_device(labels, speed, absorption, amplitude, source_x, source_y, source_z):
    anywhere = pl.BlockSpec(memory_space=pl.ANY)
    dma = pltpu.SemaphoreType.DMA
    return pl.pallas_call(
        kernel,
        out_shape=jax.ShapeDtypeStruct((2, 2, 4, 16, 256), F32),
        in_specs=[anywhere] * 9,
        out_specs=pl.BlockSpec(memory_space=pltpu.VMEM),
        scratch_shapes=[
            pltpu.VMEM((1, 8), F32),
            pltpu.VMEM((1, 8), F32),
            pltpu.VMEM((2, 2, 16), F32),
            pltpu.VMEM((2, 16), jnp.int32),
            pltpu.VMEM((2, 16), jnp.int32),
            pltpu.VMEM((2, 16), jnp.int32),
            pltpu.VMEM((12, 256, 256), BF16),
            pltpu.VMEM((7, 128, 128), F32),
            pltpu.VMEM((8, 16, 256), jnp.int32),
            pltpu.VMEM((2, 16, 256), jnp.int32),
            pltpu.VMEM((2, 2, 8, 256), jnp.int32),
            pltpu.VMEM((8, 256), jnp.int32),
            pltpu.VMEM((2, 256, 128), F32),
            pltpu.VMEM((2, 256, 128), F32),
            pltpu.VMEM((2, 256, 128), F32),
            pltpu.VMEM((2, 2, 128, 128), F32),
            pltpu.VMEM((2, 128, 256), F32),
            pltpu.VMEM((2, 8, 16, 256), F32),
            pltpu.VMEM((2, 2, 2 * CHIPS, 128), F32),
            pltpu.VMEM((2, 2, 2 * CHIPS, 128), F32),
            dma((9,)),
            dma((2, 2)),
            dma((2, 2)),
            dma((7,)),
            dma((7,)),
            dma((2,)),
            dma((2,)),
        ],
        compiler_params=pltpu.CompilerParams(
            collective_id=0, has_side_effects=True, vmem_limit_bytes=32 * 1024 * 1024
        ),
    )(*(pltpu.with_memory_space_constraint(a, pltpu.HBM) for a in (
        labels,
        speed.reshape(1, 8),
        absorption.reshape(1, 8),
        jnp.transpose(amplitude, (0, 2, 1)),
        source_x,
        source_y,
        source_z,
        jnp.asarray(transform_matrices()),
        jnp.asarray(constant_tables()),
    )))


def solution(mesh):
    return jax.shard_map(
        per_device,
        mesh=mesh,
        in_specs=(P("gx", "gy", None), P(), P(), P(), P(), P(), P()),
        out_specs=P(None, None, "gx", "gy", None),
        check_vma=False,
    )
```

```python
import functools
import math

import jax
import jax.numpy as jnp
import numpy as np
from jax import lax
from jax.experimental import pallas as pl
from jax.experimental.pallas import tpu as pltpu
from jax.sharding import PartitionSpec as P

ITERS = 4
CHIPS = 128
MESH = pl.DeviceIdType.MESH
F32 = jnp.float32
BF16 = jnp.bfloat16
WAVE = 2.0 * math.pi / 6.0
OUT, BACK = range(2)


def transform_matrices():
    def both(phase):
        c, s = np.cos(2.0 * np.pi * phase), np.sin(2.0 * np.pi * phase)
        return np.block([[c, s], [-s, c]]), np.block([[c, -s], [s, c]])

    n = np.arange(128)
    pairs = (np.arange(2)[None, :] * 128 + n[:, None]).reshape(-1)
    z_out, z_back = both((np.outer(n, n) % 128) / 128)
    high, low = n >> 4, n & 15
    mixed = ((2 * np.outer(high, high) + np.outer(low, low)) % 16) / 16
    far_out, far_back = both(mixed)
    near_back, near_out = both(mixed)
    parts = []
    for matrix in (z_out[pairs], z_back[:, pairs], far_out[:, pairs], far_back[pairs], near_out, near_back):
        high = matrix.astype(BF16)
        parts.append(high)
        parts.append((matrix - high.astype(np.float64)).astype(BF16))
    return np.stack(parts)


def constant_tables():
    n = np.arange(128)
    row, lane = n[:, None], n[None, :]
    z_turn = np.exp(-2j * np.pi * row / 256) * np.ones((1, 128))
    xy_turn = np.exp(-2j * np.pi * ((row >> 4) * (lane >> 4) / 64 + (row & 15) * (lane & 15) / 256))
    kx, ky = (row >> 4) + 8 * (lane >> 4), (row & 15) + 16 * (lane & 15)
    box = sum(np.exp(-2j * np.pi * j * kx / 64) for j in range(4)) * sum(np.exp(-2j * np.pi * j * ky / 256) for j in range(4))
    wave = [
        (2.0 * np.pi * np.where(k < size // 2, k, k - size) / size).astype(np.float32) for k, size in ((kx, 64), (ky, 256))
    ]
    tables = [z_turn.real, z_turn.imag, xy_turn.real, xy_turn.imag, box.real, box.imag]
    return np.stack([t.astype(np.float32) for t in tables] + [wave[0] * wave[0] + wave[1] * wave[1]])


def cos_turn(m):
    m = m & 255
    t = (64 - jnp.minimum(m, 256 - m)).astype(F32) * (2.0 * math.pi / 256)
    q = t * t
    poly = -1.0 / 39916800
    for term in (1.0 / 362880, -1.0 / 5040, 1.0 / 120, -1.0 / 6, 1.0):
        poly = poly * q + term
    return t * poly


def backward_turn(m):
    return cos_turn(m), -cos_turn(m - 64)


def cmul(a, b):
    return a[0] * b[0] - a[1] * b[1], a[0] * b[1] + a[1] * b[0]


def cmul_conj(a, b):
    return a[0] * b[0] + a[1] * b[1], a[1] * b[0] - a[0] * b[1]


def box_sum(m):
    w = backward_turn(m)
    square = backward_turn(2 * m)
    return cmul((1.0 + w[0], w[1]), (1.0 + square[0], square[1]))


def split(x):
    high = x.astype(BF16)
    return high, (x - high.astype(F32)).astype(BF16)


def matmul(a, b):
    dot = functools.partial(jnp.dot, preferred_element_type=F32)
    return dot(a[0], b[0]) + (dot(a[0], b[1]) + dot(a[1], b[0]))


def medium(speed, absorption):
    k = WAVE / speed
    real = k * k - absorption * absorption
    imag = 2.0 * k * absorption
    centre = 0.5 * (jnp.min(real, axis=1, keepdims=True) + jnp.max(real, axis=1, keepdims=True))
    size = jnp.sqrt((real - centre) ** 2 + imag * imag)
    return real, imag, centre, 1.05 * jnp.max(size, axis=1, keepdims=True)


def look_up(labels, table):
    out = jnp.broadcast_to(table[:, 0:1], labels.shape)
    for l in range(1, table.shape[1]):
        out = jnp.where(labels == l, table[:, l : l + 1], out)
    return out


def column(row):
    n = row.shape[1]
    eye = lax.broadcasted_iota(jnp.int32, (n, n), 0) == lax.broadcasted_iota(jnp.int32, (n, n), 1)
    spread_out = jnp.where(eye, jnp.broadcast_to(row.astype(F32), (n, n)), 0.0)
    return jnp.sum(spread_out, axis=1, keepdims=True)


def smoothed(own, x_low, x_high, y_low, y_high):
    row = lax.broadcasted_iota(jnp.int32, own.shape, 0) & 15

    def per_x(edge):
        return jnp.concatenate([jnp.broadcast_to(edge[x : x + 1], (16, 256)) for x in range(8)], axis=0)

    total = jnp.concatenate([x_low, own[:112]], axis=0) + jnp.concatenate([own[16:], x_high], axis=0)
    total = total + jnp.where(row == 0, per_x(y_low), pltpu.roll(own, 1, 0))
    total = total + jnp.where(row == 15, per_x(y_high), pltpu.roll(own, 127, 0))
    total = total + pltpu.roll(own, 1, 1) + pltpu.roll(own, 255, 1)
    return 0.5 * own + total * (1.0 / 12.0)


def farthest_first():
    offsets = [(y, x, z) for y in range(4) for x in range(4) for z in range(8)][1:]

    def hops(step, size):
        return min(step, size - step)

    return sorted(offsets, key=lambda o: (-(hops(o[0], 4) + hops(o[1], 4) + hops(o[2], 8)), hops(o[2], 8), hops(o[1], 4), o[0]))


def kernel(
    labels_hbm, speed_hbm, absorption_hbm, amplitude_hbm, sx_hbm, sy_hbm, sz_hbm, matrix_hbm, table_hbm, out,
    speed, absorption, amplitude, sx, sy, sz, matrix, table,
    labels, near_x, near_y, edge, potential, field, first, green, spectrum, result, send, recv,
    load_sem, send_sem, recv_sem, edge_send, edge_recv, half_send, half_recv,
):
    gx, gy = lax.axis_index("gx"), lax.axis_index("gy")
    core, chip_x = lax.rem(gx, 2), gx // 2
    me = chip_x * 16 + gy
    sibling = chip_x * 2 + 1 - core
    next_x, last_x = lax.rem(chip_x + 1, 8), lax.rem(chip_x + 7, 8)
    next_y, last_y = lax.rem(gy + 1, 16), lax.rem(gy + 15, 16)

    loads = [
        pltpu.make_async_copy(source, target, load_sem.at[k])
        for k, (source, target) in enumerate(
            (
                (labels_hbm, labels.at[pl.ds(4 * core, 4)]),
                (speed_hbm, speed),
                (absorption_hbm, absorption),
                (amplitude_hbm, amplitude),
                (sx_hbm, sx),
                (sy_hbm, sy),
                (sz_hbm, sz),
                (table_hbm, table),
                (matrix_hbm, matrix),
            )
        )
    ]
    for load in loads:
        load.start()

    place_y, place_x, place_z = 2 * (gy // 8) + gx // 8, lax.rem(chip_x, 4), lax.rem(gy, 8)
    ys = [lax.rem(place_y + d, 4) for d in range(4)]
    xs = [lax.rem(place_x + d, 4) for d in range(4)]
    zs = [lax.rem(place_z + d, 8) for d in range(8)]
    to_x = [[lax.rem(y, 2) * 4 + x for x in xs] for y in ys]
    to_y = [[(y // 2) * 8 + z for z in zs] for y in ys]
    order = farthest_first()

    barrier = pltpu.get_barrier_semaphore()

    def greet(device):
        pl.semaphore_signal(barrier, inc=1, device_id=device, device_id_type=MESH)

    for y, x, z in order:
        greet((2 * to_x[y][x] + core, to_y[y][z]))
    greet((sibling, gy))
    greet((2 * next_x + 1 - core, gy))
    greet((2 * last_x + 1 - core, gy))
    greet((sibling, next_y))
    greet((sibling, last_y))

    def start(stage, p):
        target = recv.at[stage, p, pl.ds(2 * me, 2)]
        for y, x, z in order:
            pltpu.make_async_remote_copy(
                src_ref=send.at[stage, p, pl.ds(2 * (to_x[y][x] * 16 + to_y[y][z]), 2)],
                dst_ref=target,
                send_sem=send_sem.at[stage, p],
                recv_sem=recv_sem.at[stage, p],
                device_id=(2 * to_x[y][x] + core, to_y[y][z]),
                device_id_type=MESH,
            ).start()
        pltpu.make_async_copy(send.at[stage, p, pl.ds(2 * me, 2)], target, recv_sem.at[stage, p]).start()

    def arrived(stage, p):
        whole = recv.at[stage, p]
        pltpu.make_async_copy(whole, whole, recv_sem.at[stage, p]).wait()

    def sent(stage, p):
        part = send.at[stage, p, pl.ds(0, 2 * CHIPS - 2)]
        pltpu.make_async_copy(part, part, send_sem.at[stage, p]).wait()

    def weights(k):
        return matrix[2 * k], matrix[2 * k + 1]

    def turns(k):
        return table[2 * k], table[2 * k + 1]

    def halves(a):
        return a[:128], a[128:]

    def sides(a):
        return a[:, :128], a[:, 128:]

    def beside(v):
        return jnp.concatenate(v, axis=1)

    def below(v):
        return jnp.concatenate(v, axis=0)

    def to_space(v):
        v = cmul_conj(sides(matmul(split(beside(v)), weights(5))), turns(1))
        return matmul(weights(3), split(below(v)))

    for load in loads[1:8]:
        load.wait()
    table_real, table_imag, centre, spread = medium(speed[...], absorption[...])
    inverse = 1.0 / spread

    def pick(ref):
        return column(jnp.where(core == 0, ref[0:1], ref[1:2]))

    corner_x, corner_y, corner_z = [pick(ref).astype(jnp.int32) for ref in (sx, sy, sz)]
    strength = tuple(column(jnp.where(core == 0, amplitude[0, k : k + 1], amplitude[1, k : k + 1])) for k in range(2))
    lane = lax.broadcasted_iota(jnp.int32, (16, 128), 1)
    high, low = lane >> 4, lane & 15
    left = below(backward_turn(4 * corner_x * high + corner_y * low)).T
    for p in range(2):
        kz = 2 * me + p
        folded = jnp.where(kz < 128, kz, kz - 256).astype(F32)
        wave_z = 2.0 * math.pi * jnp.full((1, 1), folded, F32) / 256
        shifted = (table[6] + wave_z * wave_z) - centre
        share = (1.0 / (64 * 256 * 256)) / (shifted * shifted + spread * spread)
        value = (shifted * share, spread * share)
        green[p, 0], green[p, 1] = value
        amount = cmul(strength, box_sum(jnp.full((16, 1), kz, jnp.int32)))
        q = cmul(backward_turn(32 * corner_x * high + 16 * corner_y * low + corner_z * kz), amount)
        right = below((beside(q), beside((-q[1], q[0]))))
        sums = jnp.dot(left, right, precision=lax.Precision.HIGHEST, preferred_element_type=F32)
        spectrum[p] = beside(cmul(sides(sums), cmul(value, turns(2))))
    field[...] = jnp.zeros_like(field)
    first[...] = jnp.zeros_like(first)
    loads[0].wait()
    loads[8].wait()
    for p in range(2):
        send[BACK, p] = to_space(sides(spectrum[p]))
    for x in range(4):
        edge[x : x + 1] = labels[4 * core + x, 0:1]
        edge[4 + x : 5 + x] = labels[4 * core + x, 15:16]
    pl.semaphore_wait(barrier, CHIPS - 1 + 5)

    def to_others(k, source, target, recv_index, device):
        return pltpu.make_async_remote_copy(
            src_ref=source, dst_ref=target, send_sem=edge_send.at[k], recv_sem=edge_recv.at[recv_index],
            device_id=device, device_id_type=MESH,
        )

    own = labels.at[pl.ds(4 * core, 4)]
    beside_x = lax.rem(chip_x + 7 + 2 * core, 8)
    copies = [to_others(0, own, own, 0, (sibling, gy))]
    for c in range(2):
        copies.append(
            to_others(1 + c, labels.at[7 * core], near_x.at[1 - core], 2 - core, (2 * beside_x + c, gy))
        )
        for d, to in enumerate((next_y, last_y)):
            copies.append(
                to_others(3 + 2 * d + c, edge, near_y.at[d, core], 3 + 2 * d + core, (2 * chip_x + c, to))
            )

    def medium_of_cells():
        theirs = labels.at[pl.ds(4 - 4 * core, 4)]
        landed = [theirs, near_x.at[0], near_x.at[1]] + [near_y.at[d, c] for d in range(2) for c in range(2)]
        for k, ref in enumerate(landed):
            pltpu.make_async_copy(ref, ref, edge_recv.at[k]).wait()
        for copy in copies:
            copy.wait_send()
        all_labels = labels[...].reshape(128, 256)
        y_low = below((near_y[0, 0, 4:8], near_y[0, 1, 4:8]))
        y_high = below((near_y[1, 0, 0:4], near_y[1, 1, 0:4]))
        for part, (entries, shift) in enumerate(((table_real, centre), (table_imag, spread))):
            values = [look_up(a, entries) for a in (all_labels, near_x[0], near_x[1], y_low, y_high)]
            moved = smoothed(*values) - shift
            potential[part, 0:128] = moved[:, :128].T
            potential[part, 128:256] = moved[:, 128:].T

    def iteration(step, carry):
        for p in range(2):

            @pl.when(step > 0)
            def _():
                arrived(OUT, p)
                v = cmul(halves(matmul(weights(2), split(recv[OUT, p]))), turns(1))
                v = sides(matmul(split(beside(v)), weights(4)))
                v = to_space(cmul(v, (green[p, 0], green[p, 1])))
                sent(BACK, p)
                send[BACK, p] = v

            start(BACK, p)
            if p == 0:

                @pl.when(step == 0)
                def _():
                    for copy in copies:
                        copy.start()


        @pl.when(step == 0)
        def _():
            medium_of_cells()

        arrived(BACK, 0)
        even = halves(matmul(weights(1), split(recv[BACK, 0])))
        change = [below((even[k], even[k])) + first[k] - field[k] for k in range(2)]
        moved = cmul((potential[0], potential[1]), change)
        field[0], field[1] = field[0] - moved[1] * inverse, field[1] + moved[0] * inverse
        arrived(BACK, 1)
        odd = cmul_conj(halves(matmul(weights(1), split(recv[BACK, 1]))), turns(0))
        odd = [below((odd[k], -odd[k])) for k in range(2)]
        moved = cmul((potential[0], potential[1]), odd)
        field[0], field[1] = field[0] - moved[1] * inverse, field[1] + moved[0] * inverse

        @pl.when(step == 0)
        def _():
            first[0], first[1] = [below((even[k], even[k])) + odd[k] for k in range(2)]

        @pl.when(step < ITERS - 1)
        def _():
            v = cmul((potential[0], potential[1]), (field[0], field[1]))
            upper, lower = halves(v[0]), halves(v[1])
            inputs = (
                (upper[0] + upper[1], lower[0] + lower[1]),
                cmul((upper[0] - upper[1], lower[0] - lower[1]), turns(0)),
            )
            for p in range(2):

                @pl.when(step > 0)
                def _():
                    sent(OUT, p)

                send[OUT, p] = matmul(weights(0), split(below(inputs[p])))
                start(OUT, p)

        return carry

    lax.fori_loop(0, ITERS, iteration, 0)

    copies = []
    for part in range(2):
        result[part] = beside((field[part, 0:128].T, field[part, 128:256].T)).reshape(8, 16, 256)
        copies.append(
            pltpu.make_async_remote_copy(
                src_ref=result.at[part, pl.ds(4 - 4 * core, 4)], dst_ref=out.at[core, part],
                send_sem=half_send.at[part], recv_sem=half_recv.at[part],
                device_id=(sibling, gy), device_id_type=MESH,
            )
        )
        copies[part].start()
    for part in range(2):
        out[core, part] = result[part, pl.ds(4 * core, 4)]
    for stage in range(2):
        for p in range(2):
            sent(stage, p)
    for part in range(2):
        landed = out.at[1 - core, part]
        pltpu.make_async_copy(landed, landed, half_recv.at[part]).wait()
        copies[part].wait_send()


def per_device(labels, speed, absorption, amplitude, source_x, source_y, source_z):
    anywhere = pl.BlockSpec(memory_space=pl.ANY)
    dma = pltpu.SemaphoreType.DMA
    return pl.pallas_call(
        kernel,
        out_shape=jax.ShapeDtypeStruct((2, 2, 4, 16, 256), F32),
        in_specs=[anywhere] * 9,
        out_specs=pl.BlockSpec(memory_space=pltpu.VMEM),
        scratch_shapes=[
            pltpu.VMEM((1, 8), F32),
            pltpu.VMEM((1, 8), F32),
            pltpu.VMEM((2, 2, 16), F32),
            pltpu.VMEM((2, 16), jnp.int32),
            pltpu.VMEM((2, 16), jnp.int32),
            pltpu.VMEM((2, 16), jnp.int32),
            pltpu.VMEM((12, 256, 256), BF16),
            pltpu.VMEM((7, 128, 128), F32),
            pltpu.VMEM((8, 16, 256), jnp.int32),
            pltpu.VMEM((2, 16, 256), jnp.int32),
            pltpu.VMEM((2, 2, 8, 256), jnp.int32),
            pltpu.VMEM((8, 256), jnp.int32),
            pltpu.VMEM((2, 256, 128), F32),
            pltpu.VMEM((2, 256, 128), F32),
            pltpu.VMEM((2, 256, 128), F32),
            pltpu.VMEM((2, 2, 128, 128), F32),
            pltpu.VMEM((2, 128, 256), F32),
            pltpu.VMEM((2, 8, 16, 256), F32),
            pltpu.VMEM((2, 2, 2 * CHIPS, 128), F32),
            pltpu.VMEM((2, 2, 2 * CHIPS, 128), F32),
            dma((9,)),
            dma((2, 2)),
            dma((2, 2)),
            dma((7,)),
            dma((7,)),
            dma((2,)),
            dma((2,)),
        ],
        compiler_params=pltpu.CompilerParams(
            collective_id=0, has_side_effects=True, vmem_limit_bytes=32 * 1024 * 1024
        ),
    )(*(pltpu.with_memory_space_constraint(a, pltpu.HBM) for a in (
        labels,
        speed.reshape(1, 8),
        absorption.reshape(1, 8),
        jnp.transpose(amplitude, (0, 2, 1)),
        source_x,
        source_y,
        source_z,
        jnp.asarray(transform_matrices()),
        jnp.asarray(constant_tables()),
    )))


def solution(mesh):
    return jax.shard_map(
        per_device,
        mesh=mesh,
        in_specs=(P("gx", "gy", None), P(), P(), P(), P(), P(), P()),
        out_specs=P(None, None, "gx", "gy", None),
        check_vma=False,
    )
```
